512 devices in a mesh: ctx: 32 (over z, y_lo), grp: 16 (over y_hi, x, core).
Axes of the slice: x: 4, y: 8 (y_hi: 2, y_lo: 4; y = y_hi * 4 + y_lo), z: 8, core: 2. Of those that a mesh axis runs over, the one named last changes fastest.
Arguments:
- queries: bfloat16 [16384, 8192], P('ctx', 'grp'), may hold values from -48 to 48
- kv_cols: bfloat16 [16384, 2048], P('ctx', 'grp'), may hold values from -8 to 8
- lengths: int32 [16], replicated, may hold values from 1 to 2048, 16384 in all
- page_owner: int32 [1024, 1], P('ctx'), may hold values from 0 to 31; in each aligned block of 32 rows (0 to 31, 32 to 63, ...) at most 2 rows name the same one
Outputs:
- attended: bfloat16 [16384, 8192], P('ctx', 'grp')
- decode_cache: bfloat16 [2048, 16, 2048], P('ctx', None, 'grp')
The draws below stay inside these ranges and needn't reach their ends.
Inputs may be any that keep to these rules, and one draw needn't show every extreme that they name: The lengths sum to 16384; the longest request has exactly 2048 tokens. `page_owner`: among the 32 pages of one device no owner is named more than 2 times, a bound that some block reaches.
All inputs are finite; a program needn't handle non-finite values.
Results may differ from the reference program's by a relative error of at most 0.004.
Values may be sent and summed in bfloat16 or wider, within the bound.
A program may use at most 64 MiB of HBM per device.

```python
import math
import jax
import jax.numpy as jnp
import numpy as np
from jax import lax

HD = 128
GROUP = 8
SPAN = 4
PAGE = 16
CAP = 2
TOK_DEV = 512
QH = 64
KVH = 8
SEQ = 16384
NDOCS = 16
PG_DEV = 32
NPAGES = 1024
N_CTX = 32


def key_basis(key):
    normal_part = jax.random.normal(key, (SEQ, KVH, HD), jnp.float32)
    return normal_part


def draw_kv_cols(key, part):
    basis_normal = key_basis(key)
    key = jax.random.fold_in(key, 3)
    keys_part = basis_normal
    values_part = jax.random.normal(key, (SEQ, KVH, HD), jnp.float32)
    stacked = jnp.stack([keys_part, values_part], axis=2)
    return stacked.reshape(SEQ, 2 * KVH * HD).astype(jnp.bfloat16)


def draw_queries(key, part):
    key = jax.random.fold_in(key, 5)
    first_key = jax.random.fold_in(key, 0)
    result_draw = jax.random.normal(first_key, (SEQ, KVH, GROUP, HD), jnp.float32)
    return result_draw.reshape(SEQ, KVH * GROUP * HD).astype(jnp.bfloat16)


def length_profile(count, total, limit, lean):
    portions = [(1 << 20) // math.isqrt(rank ** lean) + 1 for rank in range(2, count + 1)]
    spare, counts = total - limit - (count - 1), [1] * (count - 1)
    while spare > 0:
        candidates = [i for i in range(count - 1) if counts[i] < limit]
        pool, budget = sum([portions[i] for i in candidates]), spare
        for i in candidates:
            more = min(limit - counts[i], max(1, budget * portions[i] // pool), spare)
            counts[i] = counts[i] + more
            spare = spare - more
    return np.array([limit] + counts)


def uneven_parts(own_key, amount, total, reach, slope):
    if amount == 2:
        one = jax.random.randint(own_key, (), max(1, total - reach), min(reach, total - 1) + 1)
        return jnp.stack([one, total - one])
    tallies = jnp.asarray(length_profile(amount, total, reach, slope), jnp.int32)
    pairs = (amount - 1) // 2
    giver, taker = tallies[1:1 + 2 * pairs:2], tallies[2:2 + 2 * pairs:2]
    slack = jnp.minimum(giver - 1, reach - taker)
    moved = jax.random.randint(jax.random.fold_in(own_key, 1), (pairs,), 0, 1 << 20) % (slack + 1)
    tallies = tallies.at[1:1 + 2 * pairs:2].set(giver - moved).at[2:2 + 2 * pairs:2].set(taker + moved)
    return tallies[jax.random.permutation(jax.random.fold_in(own_key, 2), amount)]


def shared_out(stream_key, own, number, rows, number_of, top, reach, slope):
    order = jax.random.permutation(stream_key, number_of)
    heavy_load, ordinary = portions_of(number_of, rows * top, reach, slope, True), portions_of(number_of, rows * top, reach, slope, False)
    places = jnp.arange(number_of)

    def named(tallies, turn):
        used = int((tallies > 0).sum())
        fixed = max(1, used // 4)
        moved = fixed + (places - fixed + turn * (used - fixed)) % max(1, number_of - fixed)
        return jnp.zeros((number_of,), jnp.int32).at[order[jnp.where(places < fixed, places, moved)]].set(jnp.asarray(tallies, jnp.int32))

    tallies = jnp.where(number % 4 == 0, named(heavy_load, number // 4), named(ordinary, number - number // 4 - 1))
    mixed = jax.random.permutation(jax.random.fold_in(own, 3), number_of)
    donor, sink = mixed[0:number_of // 2 * 2:2], mixed[1:number_of // 2 * 2:2]
    margin = jnp.minimum(tallies[donor] - 1, reach - tallies[sink]) // 2
    margin = jnp.where((donor == order[0]) | (sink == order[0]) | (tallies[sink] == 0), 0, jnp.maximum(margin, 0))
    moved = jax.random.randint(jax.random.fold_in(own, 4), (number_of // 2,), 0, 1 << 20) % (margin + 1)
    tallies = tallies.at[donor].add(-moved).at[sink].add(moved)
    labels = jnp.searchsorted(jnp.cumsum(tallies), jnp.arange(rows * top), side="right").astype(jnp.int32)
    grid = labels.reshape(top, rows).T
    grid = grid[jax.random.permutation(jax.random.fold_in(own, 1), rows)]
    turn = jax.random.randint(jax.random.fold_in(own, 2), (rows, 1), 0, top)
    return jnp.take_along_axis(grid, (jnp.arange(top)[None, :] + turn) % top, axis=1)


def portions_of(amount, total, limit, skew, full):
    portions = [(1 << 20) // math.isqrt(grade ** skew) + 1 for grade in range(1, amount + 1)]
    largest = limit if full else min(limit, max(-(-total // amount), total * portions[0] // sum(portions)))
    least = 1 if total - largest >= amount - 1 else 0
    given, surplus = [largest] + [least] * (amount - 1), total - largest - least * (amount - 1)
    while surplus > 0:
        movable = [i for i in range(1, amount) if given[i] < largest] or [i for i in range(1, amount) if given[i] < limit]
        pool, remaining = sum([portions[i] for i in movable]), surplus
        for i in movable:
            extra = min(limit - given[i], max(1, remaining * portions[i] // pool), surplus)
            given[i] = given[i] + extra
            surplus = surplus - extra
    return np.array(given)


def setup_inputs(seed: int = 0) -> dict:
    seeds = jax.random.split(jax.random.key(seed), 5)
    queries = draw_queries(jax.random.fold_in(seeds[4], 71), 0)
    kv_cols = draw_kv_cols(jax.random.fold_in(seeds[4], 71), 0)
    lengths = uneven_parts(seeds[2], NDOCS, SEQ, SPAN * TOK_DEV, 2).astype(jnp.int32)
    page_owner_keys = jax.random.split(jax.random.fold_in(seeds[3], 1), NPAGES // PG_DEV)
    page_owner_turns = jax.random.permutation(jax.random.fold_in(seeds[3], 3), NPAGES // PG_DEV)
    page_owner = jax.vmap(lambda own, number: shared_out(jax.random.fold_in(seeds[3], 2), own, number, PG_DEV, N_CTX, 1, CAP, 1))(page_owner_keys, page_owner_turns).reshape((NPAGES, 1))
    return dict(queries=queries, kv_cols=kv_cols, lengths=lengths, page_owner=page_owner)


def segment_of(positions, doc_ends):
    return jnp.sum((doc_ends[None, :] <= positions[:, None]).astype(jnp.int32), axis=1)


def reference(queries, kv_cols, lengths, page_owner):
    doc_ends = jnp.cumsum(lengths).astype(jnp.int32)
    score_scale = HD ** -0.5
    padded = jnp.concatenate([jnp.zeros((SPAN * TOK_DEV, 2 * KVH * HD), kv_cols.dtype), kv_cols], axis=0)

    def one_block(block_index):
        query_start = (block_index * TOK_DEV).astype(jnp.int32)
        query_block = lax.dynamic_slice_in_dim(queries, query_start, TOK_DEV, 0)
        key_window = lax.dynamic_slice_in_dim(padded, query_start, (SPAN + 1) * TOK_DEV, 0)
        query_pos = query_start + jnp.arange(TOK_DEV, dtype=jnp.int32)
        key_pos = query_start - SPAN * TOK_DEV + jnp.arange((SPAN + 1) * TOK_DEV, dtype=jnp.int32)
        same_doc = segment_of(key_pos, doc_ends)[None, :] == segment_of(query_pos, doc_ends)[:, None]
        allowed = (key_pos[None, :] <= query_pos[:, None]) & (key_pos[None, :] >= 0) & same_doc
        head_outputs = []
        for kv_head in range(KVH):
            key_rows = key_window[:, 2 * kv_head * HD:(2 * kv_head + 1) * HD].astype(jnp.float32)
            value_rows = key_window[:, (2 * kv_head + 1) * HD:(2 * kv_head + 2) * HD].astype(jnp.float32)
            grouped = query_block[:, kv_head * GROUP * HD:(kv_head + 1) * GROUP * HD]
            grouped = grouped.reshape(TOK_DEV, GROUP, HD).astype(jnp.float32)
            scores = jnp.einsum("tgd,kd->gtk", grouped, key_rows) * score_scale
            scores = jnp.where(allowed[None], scores, -jnp.inf)
            row_max = jnp.max(scores, axis=2, keepdims=True)
            weights = jnp.exp(scores - row_max)
            row_total = jnp.sum(weights, axis=2, keepdims=True)
            rounded = lax.optimization_barrier(weights.astype(jnp.bfloat16)).astype(jnp.float32)
            attended_head = jnp.einsum("gtk,kd->tgd", rounded, value_rows) / jnp.transpose(row_total, (1, 0, 2))
            head_outputs.append(attended_head.reshape(TOK_DEV, GROUP * HD))
        return jnp.concatenate(head_outputs, axis=1).astype(jnp.bfloat16)

    block_outputs = lax.map(one_block, jnp.arange(N_CTX, dtype=jnp.int32))
    attended = block_outputs.reshape(SEQ, QH * HD)

    owners = page_owner[:, 0]
    onehot = (owners[:, None] == jnp.arange(N_CTX, dtype=jnp.int32)[None, :]).astype(jnp.int32)
    grouped_hot = onehot.reshape(N_CTX, PG_DEV, N_CTX)
    earlier = (jnp.cumsum(grouped_hot, axis=1) - grouped_hot).reshape(NPAGES, N_CTX)
    slot_rank = jnp.sum(earlier * onehot, axis=1)
    source_dev = jnp.arange(NPAGES, dtype=jnp.int32) // PG_DEV
    slot_index = owners * (N_CTX * CAP) + source_dev * CAP + slot_rank
    page_rows = kv_cols.reshape(NPAGES, PAGE, 2 * KVH * HD)
    decode_cache = jnp.zeros((N_CTX * N_CTX * CAP, PAGE, 2 * KVH * HD), kv_cols.dtype).at[slot_index].set(page_rows)
    return attended, decode_cache
```

```python
import functools
import math

import jax
import jax.numpy as jnp
from jax import lax
from jax.experimental import pallas as pl
from jax.experimental.pallas import tpu as pltpu
from jax.sharding import PartitionSpec as P

SPAN = 4
PAGE = 16
CAP = 2
Y = 4
CHUNKS = 2
BIG = float(2**20)
MESH = pl.DeviceIdType.MESH


def kernel(
    n_ctx, n_docs, q_ref, kv_ref, len_ref, owner_ref, att_ref, cache_ref,
    win, kaug, qaug, acc, top, outgoing,
    recv_direct, recv_partner, send_y, send_z, send_partner, recv_page, send_page, own_page,
):
    tok, hd = kv_ref.shape
    heads = q_ref.shape[1] // hd
    pages = owner_ref.shape[0]
    rows_per_owner = CAP * PAGE
    chunk = tok // CHUNKS
    scale = hd ** (-0.5) * math.log2(math.e)

    c = lax.axis_index("ctx")
    g = lax.axis_index("grp")
    a = lax.rem(c, Y)
    kind = lax.rem(g, 2)
    partner = g + 1 - 2 * kind

    barrier = pltpu.get_barrier_semaphore()

    def greet(k, carry):
        pl.semaphore_signal(barrier, inc=1, device_id=(lax.rem(c + k, n_ctx), g), device_id_type=MESH)
        return carry

    pl.semaphore_signal(barrier, inc=1, device_id=(c, partner), device_id_type=MESH)
    lax.fori_loop(1, n_ctx, greet, 0)

    win[kind, 0] = kv_ref[...]

    lane = lax.broadcasted_iota(jnp.int32, (1, hd), 1)
    starts = jnp.where(lane == n_docs, -(2**30), 2**30)
    ends = jnp.where(lane == n_docs, 0, -(2**30))
    total = jnp.int32(0)
    for doc in range(n_docs):
        starts = jnp.where(lane == doc, total, starts)
        total = total + len_ref[doc]
        ends = jnp.where(lane == doc, total, ends)
    row = lax.broadcasted_iota(jnp.int32, (tok, hd), 0)

    def in_doc(d):
        pos = row + (c - d) * tok
        return (pos >= starts) & (pos < ends)

    for d in range(SPAN + 1):
        kaug[d] = jnp.where(in_doc(d), 1.0, 0.0).astype(jnp.bfloat16)
    qaug[...] = jnp.where(in_doc(0) | (lane > n_docs), 0.0, -BIG).astype(jnp.bfloat16)

    col = lax.broadcasted_iota(jnp.int32, (pages, tok), 1)
    page = lax.broadcasted_iota(jnp.int32, (pages, tok), 0)
    owners = jnp.broadcast_to(owner_ref[...], (pages, tok))
    mine = jnp.sum(jnp.where(page == col // PAGE, owners, 0), axis=0, keepdims=True)
    rank = jnp.sum(
        jnp.where((owners == mine) & (page < col // PAGE), 1, 0), axis=0, keepdims=True
    )
    target = (mine * CAP + rank) * PAGE + lax.rem(col[:1], PAGE)
    part = 256
    for r0 in range(0, n_ctx * rows_per_owner, part):
        out_row = lax.broadcasted_iota(jnp.int32, (part, tok), 0) + r0
        pick = jnp.where(out_row == target, 1.0, 0.0).astype(jnp.bfloat16)
        outgoing[r0 : r0 + part, :] = jnp.dot(
            pick, kv_ref[...], preferred_element_type=jnp.float32
        ).astype(jnp.bfloat16)

    pl.semaphore_wait(barrier, n_ctx)

    def part_of(k, d, i):
        return win.at[k, d, pl.ds(i * chunk, chunk), :]

    def to_partner(d, i):
        return pltpu.make_async_remote_copy(
            src_ref=part_of(kind, d, i), dst_ref=part_of(kind, d, i),
            send_sem=send_partner.at[d, i], recv_sem=recv_partner.at[d, i],
            device_id=(c, partner), device_id_type=MESH,
        )

    def from_partner(d, i):
        return pltpu.make_async_remote_copy(
            src_ref=part_of(1 - kind, d, i), dst_ref=part_of(1 - kind, d, i),
            send_sem=send_partner.at[d, i], recv_sem=recv_partner.at[d, i],
            device_id=(c, partner), device_id_type=MESH,
        )

    def along_z(i):
        return pltpu.make_async_remote_copy(
            src_ref=part_of(kind, 0, i), dst_ref=part_of(kind, SPAN, i),
            send_sem=send_z.at[i], recv_sem=recv_direct.at[SPAN, i],
            device_id=(lax.rem(c + Y, n_ctx), g), device_id_type=MESH,
        )

    def along_y(d, i):
        step = jnp.where(d <= a, 1, -1)
        return pltpu.make_async_remote_copy(
            src_ref=part_of(kind, d, i), dst_ref=part_of(kind, d + step, i),
            send_sem=send_y.at[d, i], recv_sem=recv_direct.at[d + step, i],
            device_id=(c + step, g), device_id_type=MESH,
        )

    def goes_on(d):
        return jnp.where(d <= a, a < Y - 1, a > 0)

    def forward(d):
        for i in range(CHUNKS):
            pltpu.make_async_remote_copy(
                src_ref=part_of(kind, d, i), dst_ref=part_of(kind, d, i),
                send_sem=send_y.at[d, i], recv_sem=recv_direct.at[d, i],
                device_id=(c, partner), device_id_type=MESH,
            ).wait_recv()

            @pl.when(goes_on(d))
            def _():
                along_y(d, i).start()

            to_partner(d, i).start()

    def arrive(d):
        for i in range(CHUNKS):
            from_partner(d, i).wait_recv()

    for i in range(CHUNKS):
        along_z(i).start()

        @pl.when(a < Y - 1)
        def _():
            along_y(jnp.int32(0), i).start()

        to_partner(0, i).start()

    def page_copy(k):
        peer = lax.rem(c + k, n_ctx)
        return pltpu.make_async_remote_copy(
            src_ref=outgoing.at[pl.ds(peer * rows_per_owner, rows_per_owner), :],
            dst_ref=cache_ref.at[pl.ds(c * rows_per_owner, rows_per_owner), :],
            send_sem=send_page.at[k], recv_sem=recv_page.at[k],
            device_id=(peer, g), device_id_type=MESH,
        )

    def send_pages(k0, k1):
        def body(k, carry):
            page_copy(k).start()
            return carry

        lax.fori_loop(k0, k1, body, 0)

    own = pltpu.make_async_copy(
        outgoing.at[pl.ds(c * rows_per_owner, rows_per_owner), :],
        cache_ref.at[pl.ds(c * rows_per_owner, rows_per_owner), :],
        own_page,
    )
    own.start()

    ones = jnp.ones((tok, hd), jnp.bfloat16)

    def unit(d, head, r0, nr, k0, nk, causal, first, last):
        rows = slice(r0, r0 + nr)
        query = jnp.concatenate([q_ref[rows, head * hd : (head + 1) * hd], qaug[rows, :]], axis=1)
        key = jnp.concatenate([win[0, d, k0 : k0 + nk, :], kaug[d, k0 : k0 + nk, :]], axis=1)
        value = jnp.concatenate([win[1, d, k0 : k0 + nk, :], ones[:nk]], axis=1)
        scores = lax.dot_general(
            query, key, (((1,), (1,)), ((), ())), preferred_element_type=jnp.float32
        )
        if causal:
            q_pos = lax.broadcasted_iota(jnp.int32, (nr, nk), 0) + r0
            k_pos = lax.broadcasted_iota(jnp.int32, (nr, nk), 1) + k0
            scores = jnp.where(k_pos <= q_pos, scores, -BIG)
        peak = jnp.max(scores, axis=1, keepdims=True)
        if first:
            new = jnp.broadcast_to(peak, (nr, hd))
        else:
            old = top[head, rows, :]
            new = jnp.maximum(old, peak)
        wide = jnp.concatenate([new] * (nk // hd), axis=1)
        weights = jnp.exp2((scores - wide) * scale).astype(jnp.bfloat16)
        product = jnp.dot(weights, value, preferred_element_type=jnp.float32)
        if not first:
            fade = jnp.exp2((old - new) * scale)
            product = acc[head, rows, :] * jnp.concatenate([fade, fade], axis=1) + product
        if last:
            att_ref[rows, head * hd : (head + 1) * hd] = (
                product[:, :hd] / product[:, hd:]
            ).astype(jnp.bfloat16)
        else:
            acc[head, rows, :] = product
            top[head, rows, :] = new

    half = tok // 2
    arrive(0)
    for head in range(heads):
        unit(0, head, 0, half, 0, half, True, True, False)
        unit(0, head, half, half, 0, tok, True, True, False)

    forward(SPAN)
    d1 = jnp.where(a == 0, 3, 1)
    d2 = jnp.where(a == 0, 2, jnp.where(a == Y - 1, 2, 3))
    d3 = 6 - d1 - d2
    forward(d1)
    send_pages(1, n_ctx)
    arrive(SPAN)
    for head in range(heads):
        unit(SPAN, head, 0, half, 0, tok, False, False, False)
        unit(SPAN, head, half, half, half, half, False, False, False)
    for at, d in enumerate((d1, d2, d3)):
        if at > 0:
            forward(d)
        arrive(d)
        for head in range(heads):
            for r0 in (0, half):
                unit(d, head, r0, half, 0, tok, False, False, at == 2)

    for i in range(CHUNKS):
        along_z(i).wait_send()
        for d in range(SPAN + 1):
            to_partner(d, i).wait_send()

            @pl.when(goes_on(d))
            def _():
                along_y(jnp.int32(d), i).wait_send()

    def pages_done(k, carry):
        copy = page_copy(k)
        copy.wait_send()
        copy.wait_recv()
        return carry

    lax.fori_loop(1, n_ctx, pages_done, 0)
    own.wait()


def per_device(n_ctx, queries, kv_cols, lengths, page_owner):
    tok, hd = kv_cols.shape
    heads = queries.shape[1] // hd
    slots = n_ctx * CAP * PAGE
    bf16, f32 = jnp.bfloat16, jnp.float32
    vmem = pl.BlockSpec(memory_space=pltpu.VMEM)
    smem = pl.BlockSpec(memory_space=pltpu.SMEM)
    dma = pltpu.SemaphoreType.DMA
    attended, cache = pl.pallas_call(
        functools.partial(kernel, n_ctx, lengths.shape[0]),
        out_shape=(
            jax.ShapeDtypeStruct(queries.shape, bf16),
            jax.ShapeDtypeStruct((slots, hd), bf16),
        ),
        in_specs=[vmem, vmem, smem, vmem],
        out_specs=(vmem, vmem),
        scratch_shapes=[
            pltpu.VMEM((2, SPAN + 1, tok, hd), bf16),
            pltpu.VMEM((SPAN + 1, tok, hd), bf16),
            pltpu.VMEM((tok, hd), bf16),
            pltpu.VMEM((heads, tok, 2 * hd), f32),
            pltpu.VMEM((heads, tok, hd), f32),
            pltpu.VMEM((slots, hd), bf16),
            dma((SPAN + 1, CHUNKS)),
            dma((SPAN + 1, CHUNKS)),
            dma((SPAN + 1, CHUNKS)),
            dma((CHUNKS,)),
            dma((SPAN + 1, CHUNKS)),
            dma((n_ctx,)),
            dma((n_ctx,)),
            dma(()),
        ],
        compiler_params=pltpu.CompilerParams(
            collective_id=0, has_side_effects=True, vmem_limit_bytes=48 * 2**20
        ),
        cost_estimate=pl.CostEstimate(
            flops=4 * tok * heads * tok * SPAN * hd,
            bytes_accessed=4 * tok * heads * hd,
            transcendentals=tok * heads * tok * SPAN,
        ),
    )(queries, kv_cols, lengths, page_owner)
    return attended, cache.reshape(n_ctx * CAP, PAGE, hd)


def solution(mesh):
    in_specs = (P("ctx", "grp"), P("ctx", "grp"), P(), P("ctx", None))
    out_specs = (P("ctx", "grp"), P("ctx", None, "grp"))
    return jax.shard_map(
        functools.partial(per_device, mesh.shape["ctx"]),
        mesh=mesh, in_specs=in_specs, out_specs=out_specs, check_vma=False,
    )
```

```python
import functools
import math

import jax
import jax.numpy as jnp
from jax import lax
from jax.experimental import pallas as pl
from jax.experimental.pallas import tpu as pltpu
from jax.sharding import PartitionSpec as P

SPAN = 4
PAGE = 16
CAP = 2
Y = 4
CHUNKS = 4
WINDOW = 4
BIG = float(2**20)
MESH = pl.DeviceIdType.MESH


def kernel(
    n_ctx, n_docs, q_hbm, kv_hbm, len_hbm, owner_hbm, att_ref, cache_ref,
    win, far, kaug, qaug, acc, top, outgoing, q_ref, owner_ref, len_ref,
    recv_direct, recv_partner, send_own, send_on, send_partner, recv_page, send_page,
    own_page, load,
):
    tok, hd = kv_hbm.shape
    heads = q_hbm.shape[1] // hd
    pages = owner_hbm.shape[1]
    rows_per_owner = CAP * PAGE
    chunk = tok // CHUNKS
    scale = hd ** (-0.5) * math.log2(math.e)

    c = lax.axis_index("ctx")
    g = lax.axis_index("grp")
    a = lax.rem(c, Y)
    z = c // Y
    top_z = n_ctx // Y - 1
    row0 = z * Y
    kind = lax.rem(g, 2)
    partner = g + 1 - 2 * kind

    load_kv = pltpu.make_async_copy(kv_hbm, win.at[kind], load.at[0])
    load_owner = pltpu.make_async_copy(owner_hbm, owner_ref, load.at[1])
    load_len = pltpu.make_async_copy(len_hbm, len_ref, load.at[2])
    load_q = pltpu.make_async_copy(q_hbm, q_ref, load.at[3])
    load_kv.start()
    load_owner.start()
    load_len.start()
    load_q.start()

    barrier = pltpu.get_barrier_semaphore()

    def signal(semaphore, ctx, grp):
        pl.semaphore_signal(semaphore, inc=1, device_id=(ctx, grp), device_id_type=MESH)

    signal(barrier, c, partner)
    for k in range(1, Y):
        signal(barrier, row0 + lax.rem(a + k, Y), g)

    @pl.when(z > 0)
    def _():
        for k in range(Y):
            pl.when(a <= k)(functools.partial(signal, barrier, row0 - Y + k, g))

    def tell(p, carry):
        signal(barrier, p, g)
        return carry

    lax.fori_loop(row0 + Y, n_ctx, tell, 0)
    load_owner.wait()
    own = jnp.broadcast_to(owner_ref[...], (pages, pages))
    k_page = lax.broadcasted_iota(jnp.int32, (pages, pages), 0)
    i_page = lax.broadcasted_iota(jnp.int32, (pages, pages), 1)
    own_col = jnp.sum(jnp.where(k_page == i_page, own, 0), axis=1, keepdims=True)
    rank = jnp.sum(jnp.where((own_col == own) & (k_page < i_page), 1, 0), axis=0, keepdims=True)
    slot = (owner_ref[...] * CAP + rank).astype(jnp.bfloat16)
    col = lax.broadcasted_iota(jnp.int32, (pages, tok), 1)
    spread = jnp.where(
        lax.broadcasted_iota(jnp.int32, (pages, tok), 0) == col // PAGE, 1.0, 0.0
    ).astype(jnp.bfloat16)
    slot_of = jnp.dot(
        jnp.broadcast_to(slot, (16, pages)), spread, preferred_element_type=jnp.float32
    )[:1]
    target = slot_of.astype(jnp.int32) * PAGE + lax.rem(col[:1], PAGE)
    load_kv.wait()
    part = 256
    for r0 in range(0, n_ctx * rows_per_owner, part):
        out_row = lax.broadcasted_iota(jnp.int32, (part, tok), 0) + r0
        pick = jnp.where(out_row == target, 1.0, 0.0).astype(jnp.bfloat16)
        outgoing[r0 : r0 + part, :] = jnp.dot(
            pick, win[kind], preferred_element_type=jnp.float32
        ).astype(jnp.bfloat16)

    pl.semaphore_wait(barrier, Y + row0 + jnp.where(z < top_z, a + 1, 0))

    def own_chunk(i):
        return win.at[kind, pl.ds(i * chunk, chunk), :]

    def ahead(d, i):
        return pltpu.make_async_remote_copy(
            src_ref=own_chunk(i), dst_ref=far.at[kind, i, d - 1],
            send_sem=send_own.at[d, i], recv_sem=recv_direct.at[d, i],
            device_id=(c + d, g), device_id_type=MESH,
        )

    def is_ahead(d):
        far_off = (a == 0) if d == 3 else (a == Y - 1) if d == 1 else False
        return (c + d < n_ctx) & jnp.logical_not(far_off)

    def onward(i):
        step = jnp.where(a == 2, 1, -1)
        return pltpu.make_async_remote_copy(
            src_ref=far.at[kind, i, 1], dst_ref=far.at[kind, i, 1 + step],
            send_sem=send_on.at[i], recv_sem=recv_direct.at[2 + step, i],
            device_id=(c + step, g), device_id_type=MESH,
        )

    goes_on = (a == 2) | ((a == 1) & (z > 0))

    def own_to_partner(k):
        return pltpu.make_async_remote_copy(
            src_ref=win.at[k], dst_ref=win.at[k],
            send_sem=send_partner.at[CHUNKS], recv_sem=recv_partner.at[CHUNKS],
            device_id=(c, partner), device_id_type=MESH,
        )

    def far_to_partner(k, i):
        return pltpu.make_async_remote_copy(
            src_ref=far.at[k, i], dst_ref=far.at[k, i],
            send_sem=send_partner.at[i], recv_sem=recv_partner.at[i],
            device_id=(c, partner), device_id_type=MESH,
        )

    def came(d, i):
        return pltpu.make_async_remote_copy(
            src_ref=far.at[kind, i, d - 1], dst_ref=far.at[kind, i, d - 1],
            send_sem=send_own.at[d, i], recv_sem=recv_direct.at[d, i],
            device_id=(c, partner), device_id_type=MESH,
        )

    def receive(i):
        for d in (2, 1, 3, 4):
            pl.when(c >= d)(came(d, i).wait_recv)
            if d == 2:
                pl.when(goes_on)(onward(i).start)
        far_to_partner(kind, i).start()

    def send(i):
        for d in (2, 1, 3, 4):
            pl.when(is_ahead(d))(ahead(d, i).start)

    for i in range(WINDOW):
        send(i)
    own_to_partner(kind).start()

    def slots_of(p):
        return pl.ds(p * rows_per_owner, rows_per_owner)

    def page_to(p):
        return pltpu.make_async_remote_copy(
            src_ref=outgoing.at[slots_of(p), :], dst_ref=cache_ref.at[slots_of(c), :],
            send_sem=send_page.at[p], recv_sem=recv_page.at[c],
            device_id=(p, g), device_id_type=MESH,
        )

    def page_from(p):
        return pltpu.make_async_remote_copy(
            src_ref=outgoing.at[slots_of(p), :], dst_ref=cache_ref.at[slots_of(p), :],
            send_sem=send_page.at[p], recv_sem=recv_page.at[p],
            device_id=(p, g), device_id_type=MESH,
        )

    def others(first, last, act):
        def body(p, carry):
            pl.when(p != c)(functools.partial(act, p))
            return carry

        lax.fori_loop(first, last, body, 0)

    own_pages = pltpu.make_async_copy(
        outgoing.at[slots_of(c), :], cache_ref.at[slots_of(c), :], own_page
    )
    own_pages.start()

    others(0, row0 + Y, lambda p: page_to(p).start())

    load_len.wait()
    lane = lax.broadcasted_iota(jnp.int32, (1, hd), 1)
    starts = jnp.where(lane == n_docs, -(2**30), 2**30)
    ends = jnp.where(lane == n_docs, 0, -(2**30))
    total = jnp.int32(0)
    for doc in range(n_docs):
        starts = jnp.where(lane == doc, total, starts)
        total = total + len_ref[doc]
        ends = jnp.where(lane == doc, total, ends)
    row = lax.broadcasted_iota(jnp.int32, (tok, hd), 0)

    def in_doc(pos):
        return (pos >= starts) & (pos < ends)

    def one_in_doc(pos):
        return jnp.where(in_doc(pos), 1.0, 0.0).astype(jnp.bfloat16)

    here = row + c * tok
    kaug[CHUNKS] = one_in_doc(here)
    for i in range(CHUNKS):
        kaug[i] = one_in_doc((c - 1 - row // chunk) * tok + i * chunk + lax.rem(row, chunk))
    qaug[...] = jnp.where(in_doc(here) | (lane > n_docs), 0.0, -BIG).astype(jnp.bfloat16)

    for d in range(1, SPAN + 1):

        @pl.when(c < d)
        def _():
            for i in range(CHUNKS):
                far[kind, i, d - 1] = jnp.zeros((chunk, hd), jnp.bfloat16)

    load_q.wait()

    ones = jnp.ones((tok, hd), jnp.bfloat16)

    def unit(keys, values, tags, head, r0, nr, k0, causal, first, last):
        nk = keys.shape[0]
        rows = slice(r0, r0 + nr)
        query = jnp.concatenate([q_ref[rows, head * hd : (head + 1) * hd], qaug[rows, :]], axis=1)
        key = jnp.concatenate([keys, tags], axis=1)
        value = jnp.concatenate([values, ones[:nk]], axis=1)
        scores = lax.dot_general(
            query, key, (((1,), (1,)), ((), ())), preferred_element_type=jnp.float32
        )
        if causal:
            q_pos = lax.broadcasted_iota(jnp.int32, (nr, nk), 0) + r0
            k_pos = lax.broadcasted_iota(jnp.int32, (nr, nk), 1) + k0
            scores = jnp.where(k_pos <= q_pos, scores, -BIG)
        peak = jnp.max(scores, axis=1, keepdims=True)
        if first:
            new = jnp.broadcast_to(peak, (nr, hd))
        else:
            old = top[head, rows, :]
            new = jnp.maximum(old, peak)
        wide = jnp.concatenate([new] * (nk // hd), axis=1)
        weights = jnp.exp2((scores - wide) * scale).astype(jnp.bfloat16)
        product = jnp.dot(weights, value, preferred_element_type=jnp.float32)
        if not first:
            fade = jnp.exp2((old - new) * scale)
            product = acc[head, rows, :] * jnp.concatenate([fade, fade], axis=1) + product
        if last:
            att_ref[rows, head * hd : (head + 1) * hd] = (
                product[:, :hd] / product[:, hd:]
            ).astype(jnp.bfloat16)
        else:
            acc[head, rows, :] = product
            top[head, rows, :] = new

    half = tok // 2

    def diagonal(head):
        for r0, nk in ((0, half), (half, tok)):
            unit(win[0, :nk], win[1, :nk], kaug[CHUNKS, :nk], head, r0, half, 0, True, True, False)

    def earlier(i, head):
        for r0 in (0, half):
            near = SPAN if (i + 1) * chunk > r0 + 1 else SPAN - 1
            keys, values = (
                far[k, i, :near].reshape(near * chunk, hd) for k in range(2)
            )
            tags = kaug[i, : near * chunk]
            unit(keys, values, tags, head, r0, half, 0, False, False, i == CHUNKS - 1)

    own_to_partner(1 - kind).wait_recv()
    for head in range(heads):
        diagonal(head)
    receive(0)
    for i in range(CHUNKS):
        far_to_partner(1 - kind, i).wait_recv()
        for head in range(heads):
            if head == heads // 2 and i + 1 < CHUNKS:
                if i + WINDOW < CHUNKS:
                    send(i + WINDOW)
                receive(i + 1)
            earlier(i, head)

    def answer(p):
        page_from(p).wait_recv()
        page_to(p).start()

    others(row0 + Y, n_ctx, answer)

    own_to_partner(kind).wait_send()
    for i in range(CHUNKS):
        far_to_partner(kind, i).wait_send()
        for d in range(1, SPAN + 1):
            pl.when(is_ahead(d))(ahead(d, i).wait_send)
        pl.when(goes_on)(onward(i).wait_send)
    others(0, row0 + Y, lambda p: page_from(p).wait_recv())
    others(0, n_ctx, lambda p: page_to(p).wait_send())
    own_pages.wait()


def per_device(n_ctx, queries, kv_cols, lengths, page_owner):
    tok, hd = kv_cols.shape
    heads = queries.shape[1] // hd
    slots = n_ctx * CAP * PAGE
    bf16, f32 = jnp.bfloat16, jnp.float32
    vmem = pl.BlockSpec(memory_space=pltpu.VMEM)
    hbm = pl.BlockSpec(memory_space=pltpu.HBM)
    dma = pltpu.SemaphoreType.DMA
    attended, cache = pl.pallas_call(
        functools.partial(kernel, n_ctx, lengths.shape[0]),
        out_shape=(pltpu.VMEM(queries.shape, bf16), pltpu.VMEM((slots, hd), bf16)),
        in_specs=[hbm] * 4,
        out_specs=(vmem, vmem),
        scratch_shapes=[
            pltpu.VMEM((2, tok, hd), bf16),
            pltpu.VMEM((2, CHUNKS, SPAN, tok // CHUNKS, hd), bf16),
            pltpu.VMEM((CHUNKS + 1, tok, hd), bf16),
            pltpu.VMEM((tok, hd), bf16),
            pltpu.VMEM((heads, tok, 2 * hd), f32),
            pltpu.VMEM((heads, tok, hd), f32),
            pltpu.VMEM((slots, hd), bf16),
            pltpu.VMEM(queries.shape, bf16),
            pltpu.VMEM((1, page_owner.shape[0]), jnp.int32),
            pltpu.SMEM(lengths.shape, jnp.int32),
            dma((SPAN + 1, CHUNKS)),
            dma((CHUNKS + 1,)),
            dma((SPAN + 1, CHUNKS)),
            dma((CHUNKS,)),
            dma((CHUNKS + 1,)),
            dma((n_ctx,)),
            dma((n_ctx,)),
            dma(()),
            dma((4,)),
        ],
        compiler_params=pltpu.CompilerParams(
            collective_id=0, has_side_effects=True, vmem_limit_bytes=60 * 2**20
        ),
        cost_estimate=pl.CostEstimate(
            flops=4 * tok * heads * tok * SPAN * hd,
            bytes_accessed=4 * tok * heads * hd,
            transcendentals=tok * heads * tok * SPAN,
        ),
    )(queries, kv_cols, lengths, page_owner.reshape(1, -1))
    return attended, cache.reshape(n_ctx * CAP, PAGE, hd)


def solution(mesh):
    in_specs = (P("ctx", "grp"), P("ctx", "grp"), P(), P("ctx", None))
    out_specs = (P("ctx", "grp"), P("ctx", None, "grp"))
    return jax.shard_map(
        functools.partial(per_device, mesh.shape["ctx"]),
        mesh=mesh, in_specs=in_specs, out_specs=out_specs, check_vma=False,
    )
```

```python
import functools
import math

import jax
import jax.numpy as jnp
from jax import lax
from jax.experimental import pallas as pl
from jax.experimental.pallas import tpu as pltpu
from jax.sharding import PartitionSpec as P

SPAN = 4
PAGE = 16
CAP = 2
Y = 4
CHUNKS = 4
ANSWER_AT = 1
ANSWER_ROWS = 8
RELAYED = 3
BIG = float(2**20)
MESH = pl.DeviceIdType.MESH


def kernel(
    n_ctx, n_docs, q_hbm, kv_hbm, len_hbm, owner_hbm, att_ref, cache_ref,
    win, far, kaug, qaug, acc, top, outgoing, q_ref, owner_ref, len_ref,
    recv_direct, recv_partner, send_own, send_on, send_partner, recv_page, send_page,
    own_page, load,
):
    tok, hd = kv_hbm.shape
    heads = q_hbm.shape[1] // hd
    pages = owner_hbm.shape[1]
    rows_per_owner = CAP * PAGE
    chunk = tok // CHUNKS
    scale = hd ** (-0.5) * math.log2(math.e)

    c = lax.axis_index("ctx")
    g = lax.axis_index("grp")
    a = lax.rem(c, Y)
    z = c // Y
    top_z = n_ctx // Y - 1
    row0 = z * Y
    kind = lax.rem(g, 2)
    partner = g + 1 - 2 * kind

    load_kv = pltpu.make_async_copy(kv_hbm, win.at[kind], load.at[0])
    load_owner = pltpu.make_async_copy(owner_hbm, owner_ref, load.at[1])
    load_len = pltpu.make_async_copy(len_hbm, len_ref, load.at[2])
    load_q = pltpu.make_async_copy(q_hbm, q_ref, load.at[3])
    load_kv.start()
    load_owner.start()
    load_len.start()
    load_q.start()

    barrier = pltpu.get_barrier_semaphore()

    def signal(semaphore, ctx, grp):
        pl.semaphore_signal(semaphore, inc=1, device_id=(ctx, grp), device_id_type=MESH)

    signal(barrier, c, partner)
    for k in range(1, Y):
        signal(barrier, row0 + lax.rem(a + k, Y), g)

    @pl.when(z > 0)
    def _():
        for k in range(Y):
            pl.when(a <= k)(functools.partial(signal, barrier, row0 - Y + k, g))

    def tell(p, carry):
        signal(barrier, p, g)
        return carry

    lax.fori_loop(row0 + Y, n_ctx, tell, 0)
    load_owner.wait()
    own = jnp.broadcast_to(owner_ref[...], (pages, pages))
    k_page = lax.broadcasted_iota(jnp.int32, (pages, pages), 0)
    i_page = lax.broadcasted_iota(jnp.int32, (pages, pages), 1)
    own_col = jnp.sum(jnp.where(k_page == i_page, own, 0), axis=1, keepdims=True)
    rank = jnp.sum(jnp.where((own_col == own) & (k_page < i_page), 1, 0), axis=0, keepdims=True)
    slot = (owner_ref[...] * CAP + rank).astype(jnp.bfloat16)
    col = lax.broadcasted_iota(jnp.int32, (pages, tok), 1)
    spread = jnp.where(
        lax.broadcasted_iota(jnp.int32, (pages, tok), 0) == col // PAGE, 1.0, 0.0
    ).astype(jnp.bfloat16)
    slot_of = jnp.dot(
        jnp.broadcast_to(slot, (16, pages)), spread, preferred_element_type=jnp.float32
    )[:1]
    target = slot_of.astype(jnp.int32) * PAGE + lax.rem(col[:1], PAGE)
    load_kv.wait()
    part = 256
    for r0 in range(0, n_ctx * rows_per_owner, part):
        out_row = lax.broadcasted_iota(jnp.int32, (part, tok), 0) + r0
        pick = jnp.where(out_row == target, 1.0, 0.0).astype(jnp.bfloat16)
        outgoing[r0 : r0 + part, :] = jnp.dot(
            pick, win[kind], preferred_element_type=jnp.float32
        ).astype(jnp.bfloat16)

    pl.semaphore_wait(barrier, Y + row0 + jnp.where(z < top_z, a + 1, 0))

    def own_chunk(i):
        return win.at[kind, pl.ds(i * chunk, chunk), :]

    def ahead(d, i):
        return pltpu.make_async_remote_copy(
            src_ref=own_chunk(i), dst_ref=far.at[kind, i, d - 1],
            send_sem=send_own.at[d, i], recv_sem=recv_direct.at[d, i],
            device_id=(c + d, g), device_id_type=MESH,
        )

    def is_ahead(d, i):
        far_off = (a == 0) if d == 3 else (a == Y - 1) if d == 1 else False
        far_off = far_off if i < RELAYED else False
        return (c + d < n_ctx) & jnp.logical_not(far_off)

    def onward(i):
        step = jnp.where(a == 2, 1, -1)
        return pltpu.make_async_remote_copy(
            src_ref=far.at[kind, i, 1], dst_ref=far.at[kind, i, 1 + step],
            send_sem=send_on.at[i], recv_sem=recv_direct.at[2 + step, i],
            device_id=(c + step, g), device_id_type=MESH,
        )

    goes_on = (a == 2) | ((a == 1) & (z > 0))

    def own_to_partner(k):
        return pltpu.make_async_remote_copy(
            src_ref=win.at[k], dst_ref=win.at[k],
            send_sem=send_partner.at[CHUNKS], recv_sem=recv_partner.at[CHUNKS],
            device_id=(c, partner), device_id_type=MESH,
        )

    def far_to_partner(k, i):
        return pltpu.make_async_remote_copy(
            src_ref=far.at[k, i], dst_ref=far.at[k, i],
            send_sem=send_partner.at[i], recv_sem=recv_partner.at[i],
            device_id=(c, partner), device_id_type=MESH,
        )

    def came(d, i):
        return pltpu.make_async_remote_copy(
            src_ref=far.at[kind, i, d - 1], dst_ref=far.at[kind, i, d - 1],
            send_sem=send_own.at[d, i], recv_sem=recv_direct.at[d, i],
            device_id=(c, partner), device_id_type=MESH,
        )

    def receive(i):
        for d in (2, 1, 3, 4):
            pl.when(c >= d)(came(d, i).wait_recv)
            if d == 2 and i < RELAYED:
                pl.when(goes_on)(onward(i).start)
        far_to_partner(kind, i).start()

    def send(i):
        for d in (2, 1, 3, 4):
            pl.when(is_ahead(d, i))(ahead(d, i).start)

    def slots_of(p):
        return pl.ds(p * rows_per_owner, rows_per_owner)

    def page_to(p):
        return pltpu.make_async_remote_copy(
            src_ref=outgoing.at[slots_of(p), :], dst_ref=cache_ref.at[slots_of(c), :],
            send_sem=send_page, recv_sem=recv_page.at[z],
            device_id=(p, g), device_id_type=MESH,
        )

    def pages_from(row_z, count):
        return pltpu.make_async_remote_copy(
            src_ref=outgoing.at[pl.ds(0, count * rows_per_owner), :],
            dst_ref=cache_ref.at[pl.ds(row_z * Y * rows_per_owner, count * rows_per_owner), :],
            send_sem=send_page, recv_sem=recv_page.at[row_z],
            device_id=(c, partner), device_id_type=MESH,
        )

    def send_pages(first, last):
        def body(p, carry):
            pl.when(p != c)(page_to(p).start)
            return carry

        lax.fori_loop(first, last, body, 0)

    def answer(first_z, last_z):
        def body(row_z, carry):
            pages_from(row_z, Y).wait_recv()
            for k in range(Y):
                page_to(row_z * Y + k).start()
            return carry

        lax.fori_loop(first_z, last_z, body, 0)

    own_pages = pltpu.make_async_copy(
        outgoing.at[slots_of(c), :], cache_ref.at[slots_of(c), :], own_page
    )
    own_pages.start()

    send_pages(0, row0 + Y)
    own_to_partner(kind).start()
    send(0)
    send(1)

    load_len.wait()
    lane = lax.broadcasted_iota(jnp.int32, (1, hd), 1)
    starts = jnp.where(lane == n_docs, -(2**30), 2**30)
    ends = jnp.where(lane == n_docs, 0, -(2**30))
    total = jnp.int32(0)
    for doc in range(n_docs):
        starts = jnp.where(lane == doc, total, starts)
        total = total + len_ref[doc]
        ends = jnp.where(lane == doc, total, ends)
    row = lax.broadcasted_iota(jnp.int32, (tok, hd), 0)

    def in_doc(pos):
        return (pos >= starts) & (pos < ends)

    def one_in_doc(pos):
        return jnp.where(in_doc(pos), 1.0, 0.0).astype(jnp.bfloat16)

    here = row + c * tok
    kaug[CHUNKS] = one_in_doc(here)
    for i in range(CHUNKS):
        kaug[i] = one_in_doc((c - 1 - row // chunk) * tok + i * chunk + lax.rem(row, chunk))
    qaug[...] = jnp.where(in_doc(here) | (lane > n_docs), 0.0, -BIG).astype(jnp.bfloat16)

    for d in range(1, SPAN + 1):

        @pl.when(c < d)
        def _():
            for i in range(CHUNKS):
                far[kind, i, d - 1] = jnp.zeros((chunk, hd), jnp.bfloat16)

    load_q.wait()

    ones = jnp.ones((tok, hd), jnp.bfloat16)

    def unit(keys, values, tags, head, r0, nr, k0, causal, first, last):
        nk = keys.shape[0]
        rows = slice(r0, r0 + nr)
        query = jnp.concatenate([q_ref[rows, head * hd : (head + 1) * hd], qaug[rows, :]], axis=1)
        key = jnp.concatenate([keys, tags], axis=1)
        value = jnp.concatenate([values, ones[:nk]], axis=1)
        scores = lax.dot_general(
            query, key, (((1,), (1,)), ((), ())), preferred_element_type=jnp.float32
        )
        if causal:
            q_pos = lax.broadcasted_iota(jnp.int32, (nr, nk), 0) + r0
            k_pos = lax.broadcasted_iota(jnp.int32, (nr, nk), 1) + k0
            scores = jnp.where(k_pos <= q_pos, scores, -BIG)
        peak = jnp.max(scores, axis=1, keepdims=True)
        if first:
            new = jnp.broadcast_to(peak, (nr, hd))
        else:
            old = top[head, rows, :]
            new = jnp.maximum(old, peak)
        wide = jnp.concatenate([new] * (nk // hd), axis=1)
        weights = jnp.exp2((scores - wide) * scale).astype(jnp.bfloat16)
        product = jnp.dot(weights, value, preferred_element_type=jnp.float32)
        if not first:
            fade = jnp.exp2((old - new) * scale)
            product = acc[head, rows, :] * jnp.concatenate([fade, fade], axis=1) + product
        if last:
            att_ref[rows, head * hd : (head + 1) * hd] = (
                product[:, :hd] / product[:, hd:]
            ).astype(jnp.bfloat16)
        else:
            acc[head, rows, :] = product
            top[head, rows, :] = new

    half = tok // 2

    def diagonal(head):
        for r0, nk in ((0, half), (half, tok)):
            unit(win[0, :nk], win[1, :nk], kaug[CHUNKS, :nk], head, r0, half, 0, True, True, False)

    def earlier(i, head):
        for r0 in (0, half):
            near = SPAN if (i + 1) * chunk > r0 + 1 else SPAN - 1
            keys, values = (
                far[k, i, :near].reshape(near * chunk, hd) for k in range(2)
            )
            tags = kaug[i, : near * chunk]
            unit(keys, values, tags, head, r0, half, 0, False, False, i == CHUNKS - 1)

    last_z = jnp.minimum(z + 1 + ANSWER_ROWS, top_z + 1)
    own_to_partner(1 - kind).wait_recv()
    for head in range(heads):
        diagonal(head)
    receive(0)
    send(2)
    send(3)
    for i in range(CHUNKS):
        far_to_partner(1 - kind, i).wait_recv()
        for head in range(heads):
            if head == heads // 2 and i + 1 < CHUNKS:
                receive(i + 1)
            earlier(i, head)
        if i == ANSWER_AT:
            answer(z + 1, last_z)

    answer(last_z, top_z + 1)

    own_to_partner(kind).wait_send()
    for i in range(CHUNKS):
        far_to_partner(kind, i).wait_send()
        for d in range(1, SPAN + 1):
            pl.when(is_ahead(d, i))(ahead(d, i).wait_send)
        if i < RELAYED:
            pl.when(goes_on)(onward(i).wait_send)
    def pages_in(row_z, carry):
        pages_from(row_z, Y).wait_recv()
        return carry

    lax.fori_loop(0, z, pages_in, 0)
    pages_from(z, Y - 1).wait_recv()
    sent = outgoing.at[pl.ds(0, (n_ctx - 1) * rows_per_owner), :]
    pltpu.make_async_remote_copy(
        src_ref=sent, dst_ref=sent, send_sem=send_page, recv_sem=recv_page.at[z],
        device_id=(c, partner), device_id_type=MESH,
    ).wait_send()
    own_pages.wait()


def place(att_ref, cache_ref, att_out, cache_out, done):
    copies = [
        pltpu.make_async_copy(att_ref, att_out, done.at[0]),
        pltpu.make_async_copy(cache_ref, cache_out, done.at[1]),
    ]
    for copy in copies:
        copy.start()
    for copy in copies:
        copy.wait()


def per_device(n_ctx, queries, kv_cols, lengths, page_owner):
    tok, hd = kv_cols.shape
    heads = queries.shape[1] // hd
    slots = n_ctx * CAP * PAGE
    bf16, f32 = jnp.bfloat16, jnp.float32
    vmem = pl.BlockSpec(memory_space=pltpu.VMEM)
    hbm = pl.BlockSpec(memory_space=pltpu.HBM)
    dma = pltpu.SemaphoreType.DMA
    attended, cache = pl.pallas_call(
        functools.partial(kernel, n_ctx, lengths.shape[0]),
        out_shape=(pltpu.VMEM(queries.shape, bf16), pltpu.VMEM((slots, hd), bf16)),
        in_specs=[hbm] * 4,
        out_specs=(vmem, vmem),
        scratch_shapes=[
            pltpu.VMEM((2, tok, hd), bf16),
            pltpu.VMEM((2, CHUNKS, SPAN, tok // CHUNKS, hd), bf16),
            pltpu.VMEM((CHUNKS + 1, tok, hd), bf16),
            pltpu.VMEM((tok, hd), bf16),
            pltpu.VMEM((heads, tok, 2 * hd), f32),
            pltpu.VMEM((heads, tok, hd), f32),
            pltpu.VMEM((slots, hd), bf16),
            pltpu.VMEM(queries.shape, bf16),
            pltpu.VMEM((1, page_owner.shape[0]), jnp.int32),
            pltpu.SMEM(lengths.shape, jnp.int32),
            dma((SPAN + 1, CHUNKS)),
            dma((CHUNKS + 1,)),
            dma((SPAN + 1, CHUNKS)),
            dma((CHUNKS,)),
            dma((CHUNKS + 1,)),
            dma((n_ctx // Y,)),
            dma(()),
            dma(()),
            dma((4,)),
        ],
        compiler_params=pltpu.CompilerParams(
            collective_id=0, has_side_effects=True, vmem_limit_bytes=60 * 2**20
        ),
        cost_estimate=pl.CostEstimate(
            flops=4 * tok * heads * tok * SPAN * hd,
            bytes_accessed=4 * tok * heads * hd,
            transcendentals=tok * heads * tok * SPAN,
        ),
    )(queries, kv_cols, lengths, page_owner.reshape(1, -1))
    attended, cache = pl.pallas_call(
        place,
        out_shape=(
            jax.ShapeDtypeStruct(queries.shape, bf16),
            jax.ShapeDtypeStruct((slots, hd), bf16),
        ),
        in_specs=[vmem, vmem],
        out_specs=(hbm, hbm),
        scratch_shapes=[dma((2,))],
        compiler_params=pltpu.CompilerParams(vmem_limit_bytes=2**20),
    )(attended, cache)
    return attended, cache.reshape(n_ctx * CAP, PAGE, hd)


def solution(mesh):
    in_specs = (P("ctx", "grp"), P("ctx", "grp"), P(), P("ctx", None))
    out_specs = (P("ctx", "grp"), P("ctx", None, "grp"))
    return jax.shard_map(
        functools.partial(per_device, mesh.shape["ctx"]),
        mesh=mesh, in_specs=in_specs, out_specs=out_specs, check_vma=False,
    )
```

```python
import functools
import math

import jax
import jax.numpy as jnp
from jax import lax
from jax.experimental import pallas as pl
from jax.experimental.pallas import tpu as pltpu
from jax.sharding import PartitionSpec as P

SPAN = 4
PAGE = 16
CAP = 2
Y = 4
CHUNKS = 4
ANSWER_AT = 1
ANSWER_ROWS = 8
RELAYED = 1
BIG = float(2**20)
MESH = pl.DeviceIdType.MESH


def kernel(
    n_ctx, n_docs, q_hbm, kv_hbm, len_hbm, owner_hbm, att_ref, cache_ref,
    win, far, kaug, qaug, acc, top, outgoing, q_ref, owner_ref, len_ref,
    recv_direct, recv_partner, send_own, send_on, send_partner, recv_page, send_page,
    own_page, load,
):
    tok, hd = kv_hbm.shape
    heads = q_hbm.shape[1] // hd
    pages = owner_hbm.shape[1]
    rows_per_owner = CAP * PAGE
    chunk = tok // CHUNKS
    scale = hd ** (-0.5) * math.log2(math.e)

    c = lax.axis_index("ctx")
    g = lax.axis_index("grp")
    a = lax.rem(c, Y)
    z = c // Y
    top_z = n_ctx // Y - 1
    row0 = z * Y
    kind = lax.rem(g, 2)
    partner = g + 1 - 2 * kind

    load_kv = pltpu.make_async_copy(kv_hbm, win.at[kind], load.at[0])
    load_owner = pltpu.make_async_copy(owner_hbm, owner_ref, load.at[1])
    load_len = pltpu.make_async_copy(len_hbm, len_ref, load.at[2])
    load_q = pltpu.make_async_copy(q_hbm, q_ref, load.at[3])
    load_kv.start()
    load_owner.start()
    load_len.start()
    load_q.start()

    barrier = pltpu.get_barrier_semaphore()

    def signal(semaphore, ctx, grp):
        pl.semaphore_signal(semaphore, inc=1, device_id=(ctx, grp), device_id_type=MESH)

    signal(barrier, c, partner)
    for k in range(1, Y):
        signal(barrier, row0 + lax.rem(a + k, Y), g)

    @pl.when(z > 0)
    def _():
        for k in range(Y):
            pl.when(a <= k)(functools.partial(signal, barrier, row0 - Y + k, g))

    def tell(p, carry):
        signal(barrier, p, g)
        return carry

    lax.fori_loop(row0 + Y, n_ctx, tell, 0)
    load_owner.wait()
    own = jnp.broadcast_to(owner_ref[...], (pages, pages))
    k_page = lax.broadcasted_iota(jnp.int32, (pages, pages), 0)
    i_page = lax.broadcasted_iota(jnp.int32, (pages, pages), 1)
    own_col = jnp.sum(jnp.where(k_page == i_page, own, 0), axis=1, keepdims=True)
    rank = jnp.sum(jnp.where((own_col == own) & (k_page < i_page), 1, 0), axis=0, keepdims=True)
    slot = (owner_ref[...] * CAP + rank).astype(jnp.bfloat16)
    col = lax.broadcasted_iota(jnp.int32, (pages, tok), 1)
    spread = jnp.where(
        lax.broadcasted_iota(jnp.int32, (pages, tok), 0) == col // PAGE, 1.0, 0.0
    ).astype(jnp.bfloat16)
    slot_of = jnp.dot(
        jnp.broadcast_to(slot, (16, pages)), spread, preferred_element_type=jnp.float32
    )[:1]
    target = slot_of.astype(jnp.int32) * PAGE + lax.rem(col[:1], PAGE)
    load_kv.wait()
    part = 256
    for r0 in range(0, n_ctx * rows_per_owner, part):
        out_row = lax.broadcasted_iota(jnp.int32, (part, tok), 0) + r0
        pick = jnp.where(out_row == target, 1.0, 0.0).astype(jnp.bfloat16)
        outgoing[r0 : r0 + part, :] = jnp.dot(
            pick, win[kind], preferred_element_type=jnp.float32
        ).astype(jnp.bfloat16)

    pl.semaphore_wait(barrier, Y + row0 + jnp.where(z < top_z, a + 1, 0))

    def own_chunk(i):
        return win.at[kind, pl.ds(i * chunk, chunk), :]

    def ahead(d, i):
        return pltpu.make_async_remote_copy(
            src_ref=own_chunk(i), dst_ref=far.at[kind, i, d - 1],
            send_sem=send_own.at[d, i], recv_sem=recv_direct.at[d, i],
            device_id=(c + d, g), device_id_type=MESH,
        )

    def is_ahead(d, i):
        far_off = (a == 0) if d == 3 else (a == Y - 1) if d == 1 else False
        far_off = far_off if i < RELAYED else False
        return (c + d < n_ctx) & jnp.logical_not(far_off)

    def onward(i):
        step = jnp.where(a == 2, 1, -1)
        return pltpu.make_async_remote_copy(
            src_ref=far.at[kind, i, 1], dst_ref=far.at[kind, i, 1 + step],
            send_sem=send_on.at[i], recv_sem=recv_direct.at[2 + step, i],
            device_id=(c + step, g), device_id_type=MESH,
        )

    goes_on = (a == 2) | ((a == 1) & (z > 0))

    def own_to_partner(k):
        return pltpu.make_async_remote_copy(
            src_ref=win.at[k], dst_ref=win.at[k],
            send_sem=send_partner.at[CHUNKS], recv_sem=recv_partner.at[CHUNKS],
            device_id=(c, partner), device_id_type=MESH,
        )

    def far_to_partner(k, i):
        return pltpu.make_async_remote_copy(
            src_ref=far.at[k, i], dst_ref=far.at[k, i],
            send_sem=send_partner.at[i], recv_sem=recv_partner.at[i],
            device_id=(c, partner), device_id_type=MESH,
        )

    def came(d, i):
        return pltpu.make_async_remote_copy(
            src_ref=far.at[kind, i, d - 1], dst_ref=far.at[kind, i, d - 1],
            send_sem=send_own.at[d, i], recv_sem=recv_direct.at[d, i],
            device_id=(c, partner), device_id_type=MESH,
        )

    def receive(i):
        for d in (2, 1, 3, 4):
            pl.when(c >= d)(came(d, i).wait_recv)
            if d == 2 and i < RELAYED:
                pl.when(goes_on)(onward(i).start)
        far_to_partner(kind, i).start()

    def send(i):
        for d in (2, 1, 3, 4):
            pl.when(is_ahead(d, i))(ahead(d, i).start)

    def slots_of(p):
        return pl.ds(p * rows_per_owner, rows_per_owner)

    def page_to(p):
        return pltpu.make_async_remote_copy(
            src_ref=outgoing.at[slots_of(p), :], dst_ref=cache_ref.at[slots_of(c), :],
            send_sem=send_page, recv_sem=recv_page.at[z],
            device_id=(p, g), device_id_type=MESH,
        )

    def pages_from(row_z, count):
        return pltpu.make_async_remote_copy(
            src_ref=outgoing.at[pl.ds(0, count * rows_per_owner), :],
            dst_ref=cache_ref.at[pl.ds(row_z * Y * rows_per_owner, count * rows_per_owner), :],
            send_sem=send_page, recv_sem=recv_page.at[row_z],
            device_id=(c, partner), device_id_type=MESH,
        )

    def send_pages(first, last):
        def body(p, carry):
            pl.when(p != c)(page_to(p).start)
            return carry

        lax.fori_loop(first, last, body, 0)

    def answer(first_z, last_z):
        def body(row_z, carry):
            pages_from(row_z, Y).wait_recv()
            for k in range(Y):
                page_to(row_z * Y + k).start()
            return carry

        lax.fori_loop(first_z, last_z, body, 0)

    own_pages = pltpu.make_async_copy(
        outgoing.at[slots_of(c), :], cache_ref.at[slots_of(c), :], own_page
    )
    own_pages.start()

    send_pages(0, row0 + Y)
    own_to_partner(kind).start()
    send(0)
    send(1)

    load_len.wait()
    lane = lax.broadcasted_iota(jnp.int32, (1, hd), 1)
    starts = jnp.where(lane == n_docs, -(2**30), 2**30)
    ends = jnp.where(lane == n_docs, 0, -(2**30))
    total = jnp.int32(0)
    for doc in range(n_docs):
        starts = jnp.where(lane == doc, total, starts)
        total = total + len_ref[doc]
        ends = jnp.where(lane == doc, total, ends)
    row = lax.broadcasted_iota(jnp.int32, (tok, hd), 0)

    def in_doc(pos):
        return (pos >= starts) & (pos < ends)

    def one_in_doc(pos):
        return jnp.where(in_doc(pos), 1.0, 0.0).astype(jnp.bfloat16)

    here = row + c * tok
    kaug[CHUNKS] = one_in_doc(here)
    for i in range(CHUNKS):
        kaug[i] = one_in_doc((c - 1 - row // chunk) * tok + i * chunk + lax.rem(row, chunk))
    qaug[...] = jnp.where(in_doc(here) | (lane > n_docs), 0.0, -BIG).astype(jnp.bfloat16)

    for d in range(1, SPAN + 1):

        @pl.when(c < d)
        def _():
            for i in range(CHUNKS):
                far[kind, i, d - 1] = jnp.zeros((chunk, hd), jnp.bfloat16)

    load_q.wait()

    ones = jnp.ones((tok, hd), jnp.bfloat16)

    def unit(keys, values, tags, head, r0, nr, k0, causal, first, last):
        nk = keys.shape[0]
        rows = slice(r0, r0 + nr)
        query = jnp.concatenate([q_ref[rows, head * hd : (head + 1) * hd], qaug[rows, :]], axis=1)
        key = jnp.concatenate([keys, tags], axis=1)
        value = jnp.concatenate([values, ones[:nk]], axis=1)
        scores = lax.dot_general(
            query, key, (((1,), (1,)), ((), ())), preferred_element_type=jnp.float32
        )
        if causal:
            q_pos = lax.broadcasted_iota(jnp.int32, (nr, nk), 0) + r0
            k_pos = lax.broadcasted_iota(jnp.int32, (nr, nk), 1) + k0
            scores = jnp.where(k_pos <= q_pos, scores, -BIG)
        peak = jnp.max(scores, axis=1, keepdims=True)
        if first:
            new = jnp.broadcast_to(peak, (nr, hd))
        else:
            old = top[head, rows, :]
            new = jnp.maximum(old, peak)
        wide = jnp.concatenate([new] * (nk // hd), axis=1)
        weights = jnp.exp2((scores - wide) * scale).astype(jnp.bfloat16)
        product = jnp.dot(weights, value, preferred_element_type=jnp.float32)
        if not first:
            fade = jnp.exp2((old - new) * scale)
            product = acc[head, rows, :] * jnp.concatenate([fade, fade], axis=1) + product
        if last:
            att_ref[rows, head * hd : (head + 1) * hd] = (
                product[:, :hd] / product[:, hd:]
            ).astype(jnp.bfloat16)
        else:
            acc[head, rows, :] = product
            top[head, rows, :] = new

    half = tok // 2

    def diagonal(head):
        for r0, nk in ((0, half), (half, tok)):
            unit(win[0, :nk], win[1, :nk], kaug[CHUNKS, :nk], head, r0, half, 0, True, True, False)

    def earlier(i, head):
        for r0 in (0, half):
            near = SPAN if (i + 1) * chunk > r0 + 1 else SPAN - 1
            keys, values = (
                far[k, i, :near].reshape(near * chunk, hd) for k in range(2)
            )
            tags = kaug[i, : near * chunk]
            unit(keys, values, tags, head, r0, half, 0, False, False, i == CHUNKS - 1)

    last_z = jnp.minimum(z + 1 + ANSWER_ROWS, top_z + 1)
    own_to_partner(1 - kind).wait_recv()
    for head in range(heads):
        diagonal(head)
    receive(0)
    send(2)
    send(3)
    for i in range(CHUNKS):
        far_to_partner(1 - kind, i).wait_recv()
        for head in range(heads):
            if head == heads // 2 and i + 1 < CHUNKS:
                receive(i + 1)
            earlier(i, head)
        if i == ANSWER_AT:
            answer(z + 1, last_z)

    answer(last_z, top_z + 1)

    own_to_partner(kind).wait_send()
    for i in range(CHUNKS):
        far_to_partner(kind, i).wait_send()
        for d in range(1, SPAN + 1):
            pl.when(is_ahead(d, i))(ahead(d, i).wait_send)
        if i < RELAYED:
            pl.when(goes_on)(onward(i).wait_send)
    def pages_in(row_z, carry):
        pages_from(row_z, Y).wait_recv()
        return carry

    lax.fori_loop(0, z, pages_in, 0)
    pages_from(z, Y - 1).wait_recv()
    sent = outgoing.at[pl.ds(0, (n_ctx - 1) * rows_per_owner), :]
    pltpu.make_async_remote_copy(
        src_ref=sent, dst_ref=sent, send_sem=send_page, recv_sem=recv_page.at[z],
        device_id=(c, partner), device_id_type=MESH,
    ).wait_send()
    own_pages.wait()


def place(att_ref, cache_ref, att_out, cache_out, done):
    copies = [
        pltpu.make_async_copy(att_ref, att_out, done.at[0]),
        pltpu.make_async_copy(cache_ref, cache_out, done.at[1]),
    ]
    for copy in copies:
        copy.start()
    for copy in copies:
        copy.wait()


def per_device(n_ctx, queries, kv_cols, lengths, page_owner):
    tok, hd = kv_cols.shape
    heads = queries.shape[1] // hd
    slots = n_ctx * CAP * PAGE
    bf16, f32 = jnp.bfloat16, jnp.float32
    vmem = pl.BlockSpec(memory_space=pltpu.VMEM)
    hbm = pl.BlockSpec(memory_space=pltpu.HBM)
    dma = pltpu.SemaphoreType.DMA
    attended, cache = pl.pallas_call(
        functools.partial(kernel, n_ctx, lengths.shape[0]),
        out_shape=(pltpu.VMEM(queries.shape, bf16), pltpu.VMEM((slots, hd), bf16)),
        in_specs=[hbm] * 4,
        out_specs=(vmem, vmem),
        scratch_shapes=[
            pltpu.VMEM((2, tok, hd), bf16),
            pltpu.VMEM((2, CHUNKS, SPAN, tok // CHUNKS, hd), bf16),
            pltpu.VMEM((CHUNKS + 1, tok, hd), bf16),
            pltpu.VMEM((tok, hd), bf16),
            pltpu.VMEM((heads, tok, 2 * hd), f32),
            pltpu.VMEM((heads, tok, hd), f32),
            pltpu.VMEM((slots, hd), bf16),
            pltpu.VMEM(queries.shape, bf16),
            pltpu.VMEM((1, page_owner.shape[0]), jnp.int32),
            pltpu.SMEM(lengths.shape, jnp.int32),
            dma((SPAN + 1, CHUNKS)),
            dma((CHUNKS + 1,)),
            dma((SPAN + 1, CHUNKS)),
            dma((CHUNKS,)),
            dma((CHUNKS + 1,)),
            dma((n_ctx // Y,)),
            dma(()),
            dma(()),
            dma((4,)),
        ],
        compiler_params=pltpu.CompilerParams(
            collective_id=0, has_side_effects=True, vmem_limit_bytes=60 * 2**20
        ),
        cost_estimate=pl.CostEstimate(
            flops=4 * tok * heads * tok * SPAN * hd,
            bytes_accessed=4 * tok * heads * hd,
            transcendentals=tok * heads * tok * SPAN,
        ),
    )(queries, kv_cols, lengths, page_owner.reshape(1, -1))
    attended, cache = pl.pallas_call(
        place,
        out_shape=(
            jax.ShapeDtypeStruct(queries.shape, bf16),
            jax.ShapeDtypeStruct((slots, hd), bf16),
        ),
        in_specs=[vmem, vmem],
        out_specs=(hbm, hbm),
        scratch_shapes=[dma((2,))],
        compiler_params=pltpu.CompilerParams(vmem_limit_bytes=2**20),
    )(attended, cache)
    return attended, cache.reshape(n_ctx * CAP, PAGE, hd)


def solution(mesh):
    in_specs = (P("ctx", "grp"), P("ctx", "grp"), P(), P("ctx", None))
    out_specs = (P("ctx", "grp"), P("ctx", None, "grp"))
    return jax.shard_map(
        functools.partial(per_device, mesh.shape["ctx"]),
        mesh=mesh, in_specs=in_specs, out_specs=out_specs, check_vma=False,
    )
```

```python
import functools
import math

import jax
import jax.numpy as jnp
from jax import lax
from jax.experimental import pallas as pl
from jax.experimental.pallas import tpu as pltpu
from jax.sharding import PartitionSpec as P

SPAN = 4
PAGE = 16
CAP = 2
Y = 4
CHUNKS = 4
ANSWER_AT = 1
ANSWER_ROWS = 8
RELAYED = 1
BIG = float(2**20)
MESH = pl.DeviceIdType.MESH


def kernel(
    n_ctx, n_docs, q_hbm, kv_hbm, len_hbm, owner_hbm, att_ref, cache_ref,
    win, far, kaug, qaug, acc, top, outgoing, q_ref, owner_ref, len_ref,
    recv_direct, recv_partner, send_own, send_on, send_partner, recv_page, send_page,
    own_page, load,
):
    tok, hd = kv_hbm.shape
    heads = q_hbm.shape[1] // hd
    pages = owner_hbm.shape[1]
    rows_per_owner = CAP * PAGE
    chunk = tok // CHUNKS
    scale = hd ** (-0.5) * math.log2(math.e)

    c = lax.axis_index("ctx")
    g = lax.axis_index("grp")
    a = lax.rem(c, Y)
    z = c // Y
    top_z = n_ctx // Y - 1
    row0 = z * Y
    kind = lax.rem(g, 2)
    partner = g + 1 - 2 * kind

    load_kv = pltpu.make_async_copy(kv_hbm, win.at[kind], load.at[0])
    load_owner = pltpu.make_async_copy(owner_hbm, owner_ref, load.at[1])
    load_len = pltpu.make_async_copy(len_hbm, len_ref, load.at[2])
    load_q = pltpu.make_async_copy(q_hbm, q_ref, load.at[3])
    load_kv.start()
    load_owner.start()
    load_len.start()
    load_q.start()

    barrier = pltpu.get_barrier_semaphore()

    def signal(semaphore, ctx, grp):
        pl.semaphore_signal(semaphore, inc=1, device_id=(ctx, grp), device_id_type=MESH)

    signal(barrier, c, partner)
    for k in range(1, Y):
        signal(barrier, row0 + lax.rem(a + k, Y), g)

    @pl.when(z > 0)
    def _():
        for k in range(Y):
            pl.when(a <= k)(functools.partial(signal, barrier, row0 - Y + k, g))

    def tell(p, carry):
        signal(barrier, p, g)
        return carry

    lax.fori_loop(row0 + Y, n_ctx, tell, 0)
    load_owner.wait()
    own = jnp.broadcast_to(owner_ref[...], (pages, pages))
    k_page = lax.broadcasted_iota(jnp.int32, (pages, pages), 0)
    i_page = lax.broadcasted_iota(jnp.int32, (pages, pages), 1)
    own_col = jnp.sum(jnp.where(k_page == i_page, own, 0), axis=1, keepdims=True)
    rank = jnp.sum(jnp.where((own_col == own) & (k_page < i_page), 1, 0), axis=0, keepdims=True)
    slot = (owner_ref[...] * CAP + rank).astype(jnp.bfloat16)
    col = lax.broadcasted_iota(jnp.int32, (pages, tok), 1)
    spread = jnp.where(
        lax.broadcasted_iota(jnp.int32, (pages, tok), 0) == col // PAGE, 1.0, 0.0
    ).astype(jnp.bfloat16)
    slot_of = jnp.dot(
        jnp.broadcast_to(slot, (16, pages)), spread, preferred_element_type=jnp.float32
    )[:1]
    target = slot_of.astype(jnp.int32) * PAGE + lax.rem(col[:1], PAGE)
    load_kv.wait()
    part = 256
    for r0 in range(0, n_ctx * rows_per_owner, part):
        out_row = lax.broadcasted_iota(jnp.int32, (part, tok), 0) + r0
        pick = jnp.where(out_row == target, 1.0, 0.0).astype(jnp.bfloat16)
        outgoing[r0 : r0 + part, :] = jnp.dot(
            pick, win[kind], preferred_element_type=jnp.float32
        ).astype(jnp.bfloat16)

    pl.semaphore_wait(barrier, Y + row0 + jnp.where(z < top_z, a + 1, 0))

    def own_chunk(i):
        return win.at[kind, pl.ds(i * chunk, chunk), :]

    def ahead(d, i):
        return pltpu.make_async_remote_copy(
            src_ref=own_chunk(i), dst_ref=far.at[kind, i, d - 1],
            send_sem=send_own.at[d, i], recv_sem=recv_direct.at[d, i],
            device_id=(c + d, g), device_id_type=MESH,
        )

    def is_ahead(d, i):
        far_off = (a == 0) if d == 3 else (a == Y - 1) if d == 1 else False
        far_off = far_off if i < RELAYED else False
        return (c + d < n_ctx) & jnp.logical_not(far_off)

    def onward(i):
        step = jnp.where(a == 2, 1, -1)
        return pltpu.make_async_remote_copy(
            src_ref=far.at[kind, i, 1], dst_ref=far.at[kind, i, 1 + step],
            send_sem=send_on.at[i], recv_sem=recv_direct.at[2 + step, i],
            device_id=(c + step, g), device_id_type=MESH,
        )

    goes_on = (a == 2) | ((a == 1) & (z > 0))

    def own_to_partner(k):
        return pltpu.make_async_remote_copy(
            src_ref=win.at[k], dst_ref=win.at[k],
            send_sem=send_partner.at[CHUNKS], recv_sem=recv_partner.at[CHUNKS],
            device_id=(c, partner), device_id_type=MESH,
        )

    def far_to_partner(k, i):
        return pltpu.make_async_remote_copy(
            src_ref=far.at[k, i], dst_ref=far.at[k, i],
            send_sem=send_partner.at[i], recv_sem=recv_partner.at[i],
            device_id=(c, partner), device_id_type=MESH,
        )

    def came(d, i):
        return pltpu.make_async_remote_copy(
            src_ref=far.at[kind, i, d - 1], dst_ref=far.at[kind, i, d - 1],
            send_sem=send_own.at[d, i], recv_sem=recv_direct.at[d, i],
            device_id=(c, partner), device_id_type=MESH,
        )

    def receive(i):
        for d in (2, 1, 3, 4):
            pl.when(c >= d)(came(d, i).wait_recv)
            if d == 2 and i < RELAYED:
                pl.when(goes_on)(onward(i).start)
        far_to_partner(kind, i).start()

    def send(i):
        for d in (2, 1, 3, 4):
            pl.when(is_ahead(d, i))(ahead(d, i).start)

    def slots_of(p):
        return pl.ds(p * rows_per_owner, rows_per_owner)

    def page_to(p):
        return pltpu.make_async_remote_copy(
            src_ref=outgoing.at[slots_of(p), :], dst_ref=cache_ref.at[slots_of(c), :],
            send_sem=send_page, recv_sem=recv_page.at[z],
            device_id=(p, g), device_id_type=MESH,
        )

    def pages_from(row_z, count):
        return pltpu.make_async_remote_copy(
            src_ref=outgoing.at[pl.ds(0, count * rows_per_owner), :],
            dst_ref=cache_ref.at[pl.ds(row_z * Y * rows_per_owner, count * rows_per_owner), :],
            send_sem=send_page, recv_sem=recv_page.at[row_z],
            device_id=(c, partner), device_id_type=MESH,
        )

    def send_pages(first, last):
        def body(p, carry):
            pl.when(p != c)(page_to(p).start)
            return carry

        lax.fori_loop(first, last, body, 0)

    def answer(first_z, last_z):
        def body(row_z, carry):
            pages_from(row_z, Y).wait_recv()
            for k in range(Y):
                page_to(row_z * Y + k).start()
            return carry

        lax.fori_loop(first_z, last_z, body, 0)

    own_pages = pltpu.make_async_copy(
        outgoing.at[slots_of(c), :], cache_ref.at[slots_of(c), :], own_page
    )
    own_pages.start()

    own_to_partner(kind).start()
    send_pages(0, row0 + Y)
    send(0)
    send(1)

    load_len.wait()
    lane = lax.broadcasted_iota(jnp.int32, (1, hd), 1)
    starts = jnp.where(lane == n_docs, -(2**30), 2**30)
    ends = jnp.where(lane == n_docs, 0, -(2**30))
    total = jnp.int32(0)
    for doc in range(n_docs):
        starts = jnp.where(lane == doc, total, starts)
        total = total + len_ref[doc]
        ends = jnp.where(lane == doc, total, ends)
    row = lax.broadcasted_iota(jnp.int32, (tok, hd), 0)

    def in_doc(pos):
        return (pos >= starts) & (pos < ends)

    def one_in_doc(pos):
        return jnp.where(in_doc(pos), 1.0, 0.0).astype(jnp.bfloat16)

    here = row + c * tok
    kaug[CHUNKS] = one_in_doc(here)
    for i in range(CHUNKS):
        kaug[i] = one_in_doc((c - 1 - row // chunk) * tok + i * chunk + lax.rem(row, chunk))
    qaug[...] = jnp.where(in_doc(here) | (lane > n_docs), 0.0, -BIG).astype(jnp.bfloat16)

    for d in range(1, SPAN + 1):

        @pl.when(c < d)
        def _():
            for i in range(CHUNKS):
                far[kind, i, d - 1] = jnp.zeros((chunk, hd), jnp.bfloat16)

    load_q.wait()

    ones = jnp.ones((tok, hd), jnp.bfloat16)

    def unit(keys, values, tags, head, r0, nr, k0, causal, first, last):
        nk = keys.shape[0]
        rows = slice(r0, r0 + nr)
        query = jnp.concatenate([q_ref[rows, head * hd : (head + 1) * hd], qaug[rows, :]], axis=1)
        key = jnp.concatenate([keys, tags], axis=1)
        value = jnp.concatenate([values, ones[:nk]], axis=1)
        scores = lax.dot_general(
            query, key, (((1,), (1,)), ((), ())), preferred_element_type=jnp.float32
        )
        if causal:
            q_pos = lax.broadcasted_iota(jnp.int32, (nr, nk), 0) + r0
            k_pos = lax.broadcasted_iota(jnp.int32, (nr, nk), 1) + k0
            scores = jnp.where(k_pos <= q_pos, scores, -BIG)
        peak = jnp.max(scores, axis=1, keepdims=True)
        if first:
            new = jnp.broadcast_to(peak, (nr, hd))
        else:
            old = top[head, rows, :]
            new = jnp.maximum(old, peak)
        wide = jnp.concatenate([new] * (nk // hd), axis=1)
        weights = jnp.exp2((scores - wide) * scale).astype(jnp.bfloat16)
        product = jnp.dot(weights, value, preferred_element_type=jnp.float32)
        if not first:
            fade = jnp.exp2((old - new) * scale)
            product = acc[head, rows, :] * jnp.concatenate([fade, fade], axis=1) + product
        if last:
            att_ref[rows, head * hd : (head + 1) * hd] = (
                product[:, :hd] / product[:, hd:]
            ).astype(jnp.bfloat16)
        else:
            acc[head, rows, :] = product
            top[head, rows, :] = new

    half = tok // 2

    def diagonal(head):
        for r0, nk in ((0, half), (half, tok)):
            unit(win[0, :nk], win[1, :nk], kaug[CHUNKS, :nk], head, r0, half, 0, True, True, False)

    def earlier(i, head):
        for r0 in (0, half):
            near = SPAN if (i + 1) * chunk > r0 + 1 else SPAN - 1
            keys, values = (
                far[k, i, :near].reshape(near * chunk, hd) for k in range(2)
            )
            tags = kaug[i, : near * chunk]
            unit(keys, values, tags, head, r0, half, 0, False, False, i == CHUNKS - 1)

    last_z = jnp.minimum(z + 1 + ANSWER_ROWS, top_z + 1)
    own_to_partner(1 - kind).wait_recv()
    for head in range(heads):
        diagonal(head)
    receive(0)
    send(2)
    send(3)
    for i in range(CHUNKS):
        far_to_partner(1 - kind, i).wait_recv()
        for head in range(heads):
            if head == 1 and i + 1 < CHUNKS:
                receive(i + 1)
            earlier(i, head)
        if i == ANSWER_AT:
            answer(z + 1, last_z)

    answer(last_z, top_z + 1)

    own_to_partner(kind).wait_send()
    for i in range(CHUNKS):
        far_to_partner(kind, i).wait_send()
        for d in range(1, SPAN + 1):
            pl.when(is_ahead(d, i))(ahead(d, i).wait_send)
        if i < RELAYED:
            pl.when(goes_on)(onward(i).wait_send)
    def pages_in(row_z, carry):
        pages_from(row_z, Y).wait_recv()
        return carry

    lax.fori_loop(0, z, pages_in, 0)
    pages_from(z, Y - 1).wait_recv()
    sent = outgoing.at[pl.ds(0, (n_ctx - 1) * rows_per_owner), :]
    pltpu.make_async_remote_copy(
        src_ref=sent, dst_ref=sent, send_sem=send_page, recv_sem=recv_page.at[z],
        device_id=(c, partner), device_id_type=MESH,
    ).wait_send()
    own_pages.wait()


def place(att_ref, cache_ref, att_out, cache_out, done):
    copies = [
        pltpu.make_async_copy(att_ref, att_out, done.at[0]),
        pltpu.make_async_copy(cache_ref, cache_out, done.at[1]),
    ]
    for copy in copies:
        copy.start()
    for copy in copies:
        copy.wait()


def per_device(n_ctx, queries, kv_cols, lengths, page_owner):
    tok, hd = kv_cols.shape
    heads = queries.shape[1] // hd
    slots = n_ctx * CAP * PAGE
    bf16, f32 = jnp.bfloat16, jnp.float32
    vmem = pl.BlockSpec(memory_space=pltpu.VMEM)
    hbm = pl.BlockSpec(memory_space=pltpu.HBM)
    dma = pltpu.SemaphoreType.DMA
    attended, cache = pl.pallas_call(
        functools.partial(kernel, n_ctx, lengths.shape[0]),
        out_shape=(pltpu.VMEM(queries.shape, bf16), pltpu.VMEM((slots, hd), bf16)),
        in_specs=[hbm] * 4,
        out_specs=(vmem, vmem),
        scratch_shapes=[
            pltpu.VMEM((2, tok, hd), bf16),
            pltpu.VMEM((2, CHUNKS, SPAN, tok // CHUNKS, hd), bf16),
            pltpu.VMEM((CHUNKS + 1, tok, hd), bf16),
            pltpu.VMEM((tok, hd), bf16),
            pltpu.VMEM((heads, tok, 2 * hd), f32),
            pltpu.VMEM((heads, tok, hd), f32),
            pltpu.VMEM((slots, hd), bf16),
            pltpu.VMEM(queries.shape, bf16),
            pltpu.VMEM((1, page_owner.shape[0]), jnp.int32),
            pltpu.SMEM(lengths.shape, jnp.int32),
            dma((SPAN + 1, CHUNKS)),
            dma((CHUNKS + 1,)),
            dma((SPAN + 1, CHUNKS)),
            dma((CHUNKS,)),
            dma((CHUNKS + 1,)),
            dma((n_ctx // Y,)),
            dma(()),
            dma(()),
            dma((4,)),
        ],
        compiler_params=pltpu.CompilerParams(
            collective_id=0, has_side_effects=True, vmem_limit_bytes=60 * 2**20
        ),
        cost_estimate=pl.CostEstimate(
            flops=4 * tok * heads * tok * SPAN * hd,
            bytes_accessed=4 * tok * heads * hd,
            transcendentals=tok * heads * tok * SPAN,
        ),
    )(queries, kv_cols, lengths, page_owner.reshape(1, -1))
    attended, cache = pl.pallas_call(
        place,
        out_shape=(
            jax.ShapeDtypeStruct(queries.shape, bf16),
            jax.ShapeDtypeStruct((slots, hd), bf16),
        ),
        in_specs=[vmem, vmem],
        out_specs=(hbm, hbm),
        scratch_shapes=[dma((2,))],
        compiler_params=pltpu.CompilerParams(vmem_limit_bytes=2**20),
    )(attended, cache)
    return attended, cache.reshape(n_ctx * CAP, PAGE, hd)


def solution(mesh):
    in_specs = (P("ctx", "grp"), P("ctx", "grp"), P(), P("ctx", None))
    out_specs = (P("ctx", "grp"), P("ctx", None, "grp"))
    return jax.shard_map(
        functools.partial(per_device, mesh.shape["ctx"]),
        mesh=mesh, in_specs=in_specs, out_specs=out_specs, check_vma=False,
    )
```
